512 devices in a mesh: gy: 16 (over x, z_lo), gx: 32 (over y, z_hi, core).
Axes of the slice: x: 4, y: 4, z: 16 (z_hi: 4, z_lo: 4; z = z_hi * 4 + z_lo), core: 2. Of those that a mesh axis runs over, the one named last changes fastest.
Arguments:
- field: bfloat16 [256, 256, 1024], P('gx', 'gy'), may hold values from -6 to 6
- center_block: bfloat16 [64, 64], replicated, may hold values from -0.75 to 0.75
- couple_blocks: bfloat16 [6, 64, 64], replicated, may hold values from -0.75 to 0.75
- cell_index: int32 [16, 32, 32, 32], P('gy', 'gx'), may hold values from 0 to 2047, as said below
- slot_counts: int32 [16, 32, 32], P('gy', 'gx'), may hold values from 0 to 32, as said below
- assays: bfloat16 [16, 32, 32, 2048], P('gy', 'gx'), may hold values from -6 to 6
- assay_weights: bfloat16 [16, 32, 32, 2048], P('gy', 'gx'), may hold values from 0.5 to 4
Outputs:
- gradient: bfloat16 [256, 256, 1024], P('gx', 'gy')
The draws below stay inside these ranges and needn't reach their ends.
Inputs may be any that keep to these rules, and one draw needn't show every extreme that they name: `cell_index`: local cell numbers within the destination tile, every slot holds a valid one. `slot_counts`: composites of a list; some list is full, and some tile receives full lists from every owner of its band.
All inputs are finite; a program needn't handle non-finite values.
Results may differ from the reference program's by a relative error of at most 0.0039.
Values may be sent and summed in bfloat16 or wider, within the bound.
A program may use at most 64 MiB of HBM per device.

```python
import math
import jax
import jax.numpy as jnp
from jax import lax

CX = 8
CY = 16
NZ = 16
ELEMS = 64
SLOT = 32
TILES = 32
BANDS = 16
NX = 256
NY = 256
CELLS = 2048


def draw_cell_index(key, part):
    base = jax.random.fold_in(key, 11)
    first, second = jax.random.split(base)
    shape = (BANDS, TILES, TILES, SLOT)
    values = jax.random.randint(first, shape, 0, CELLS, dtype=jnp.int32).reshape(-1)
    spots = jax.random.randint(second, (2,), 0, values.shape[0], dtype=jnp.int32)
    positions = jnp.arange(values.shape[0], dtype=jnp.int32)
    values = jnp.where(positions == spots[0], CELLS - 1, values)
    values = jnp.where((positions == spots[1]) & (spots[1] != spots[0]), 0, values)
    return values.reshape(shape)


def draw_slot_counts(key, part):
    base = jax.random.fold_in(key, 23)
    cap_key, count_key, pick_key = jax.random.split(base, 3)
    caps = jax.random.randint(cap_key, (BANDS, 1, TILES), SLOT // 8, SLOT + 1, dtype=jnp.int32)
    counts = jax.random.randint(count_key, (BANDS, TILES, TILES), caps // 2, caps + 1, dtype=jnp.int32)
    pick = jax.random.randint(pick_key, (2,), 0, BANDS * TILES, dtype=jnp.int32)
    band_pick = pick[0] // TILES
    tile_pick = pick[0] % TILES
    band_rows = jnp.arange(BANDS, dtype=jnp.int32)[:, None, None]
    tile_cols = jnp.arange(TILES, dtype=jnp.int32)[None, None, :]
    full = (band_rows == band_pick) & (tile_cols == tile_pick)
    return jnp.where(full, SLOT, counts).astype(jnp.int32)


def level_of(rng, shape, shards, smallest, top_value):
    gain, own = 1.0, jax.random.fold_in(rng, 6)
    for dim, blocks in shards:
        steps = jnp.exp(jax.random.uniform(jax.random.fold_in(own, dim), (blocks,), jnp.float32, smallest / len(shards), top_value / len(shards)))
        gain = gain * jnp.repeat(steps, shape[dim] // blocks).reshape([-1 if axis == dim else 1 for axis in range(len(shape))])
    return gain


def centred(rng, extent, scale, bound, cuts=(), kind=jnp.bfloat16):
    factor_of = level_of(rng, extent, cuts, -0.22, 0.18) if cuts else 1.0
    drawn = jax.random.normal(rng, extent, jnp.float32) * scale * factor_of
    return jnp.minimum(jnp.maximum(drawn, -bound), bound).astype(kind)


def setup_inputs(seed: int = 0) -> dict:
    streams_of = jax.random.split(jax.random.key(seed), 8)
    field = centred(streams_of[0], (NX, NY, NZ * ELEMS), 1.0, 6.0, ((0, 32), (1, 16)))
    center_block = centred(streams_of[1], (ELEMS, ELEMS), ELEMS ** -0.5, 0.75)
    couple_blocks = centred(streams_of[2], (6, ELEMS, ELEMS), ELEMS ** -0.5, 0.75)
    cell_index = draw_cell_index(jax.random.fold_in(streams_of[7], 71), 0)
    slot_counts = draw_slot_counts(jax.random.fold_in(streams_of[7], 71), 0)
    assays = centred(streams_of[5], (BANDS, TILES, TILES, SLOT * ELEMS), 1.0, 6.0, ((0, 16), (1, 32)))
    assay_weights = jnp.clip(jnp.exp(math.log(4.0) - 2.0794415 * jax.random.uniform(streams_of[6], (BANDS, TILES, TILES, SLOT * ELEMS), jnp.float32) ** level_of(streams_of[6], (BANDS, TILES, TILES, SLOT * ELEMS), ((0, 16), (1, 32)), -0.2, 0.2)), 0.5, 4.0).astype(jnp.bfloat16)
    return {"field": field, "center_block": center_block, "couple_blocks": couple_blocks, "cell_index": cell_index, "slot_counts": slot_counts, "assays": assays, "assay_weights": assay_weights}


def stencil(block, center, couple, form, flip):
    middle = block[1:-1, 1:-1, 1:-1]
    plus_x, minus_x = block[2:, 1:-1, 1:-1], block[:-2, 1:-1, 1:-1]
    plus_y, minus_y = block[1:-1, 2:, 1:-1], block[1:-1, :-2, 1:-1]
    plus_z, minus_z = block[1:-1, 1:-1, 2:], block[1:-1, 1:-1, :-2]
    if flip:
        nearby = (minus_x, plus_x, minus_y, plus_y, minus_z, plus_z)
    else:
        nearby = (plus_x, minus_x, plus_y, minus_y, plus_z, minus_z)
    total = jnp.einsum(form, middle, center)
    for which in range(6):
        total = total - jnp.einsum(form, nearby[which], couple[which])
    return total


def reference(field, center_block, couple_blocks, cell_index, slot_counts, assays, assay_weights):
    whole = field.reshape(NX, NY, NZ, ELEMS)
    center = center_block.astype(jnp.float32)
    couple = couple_blocks.astype(jnp.float32)
    padded_u = jnp.pad(whole, ((1, 1), (1, 1), (1, 1), (0, 0)))
    starts = jnp.arange(TILES, dtype=jnp.int32) * CX

    def forward_block(start):
        block = lax.dynamic_slice_in_dim(padded_u, start, CX + 2, 0).astype(jnp.float32)
        return stencil(block, center, couple, "xyze,ef->xyzf", False).astype(jnp.bfloat16)

    image = lax.map(forward_block, starts).reshape(NX, NY, NZ, ELEMS)
    padded_w = jnp.pad(image, ((1, 1), (1, 1), (1, 1), (0, 0)))
    band_ids = jnp.arange(BANDS, dtype=jnp.int32)[:, None, None]
    slot_ids = jnp.arange(SLOT, dtype=jnp.int32)[None, None, :]

    def final_block(tile):
        start = tile * CX
        block = lax.dynamic_slice_in_dim(padded_w, start, CX + 2, 0).astype(jnp.float32)
        prior = stencil(block, center, couple, "xyze,fe->xyzf", True)
        local = cell_index[:, :, tile, :]
        row_x = local // (CY * NZ)
        row_y = (local // NZ) % CY
        row_z = local % NZ
        values = whole[start + row_x, band_ids * CY + row_y, row_z].astype(jnp.float32)
        target = assays[:, :, tile].reshape(BANDS, TILES, SLOT, ELEMS).astype(jnp.float32)
        scale = assay_weights[:, :, tile].reshape(BANDS, TILES, SLOT, ELEMS).astype(jnp.float32)
        used = slot_ids < slot_counts[:, :, tile][:, :, None]
        misfit = jnp.where(used[..., None], scale * (target - values), jnp.float32(0.0))
        band_full = jnp.broadcast_to(band_ids, local.shape)
        data = jnp.zeros((BANDS, CELLS, ELEMS), jnp.float32).at[band_full, local].add(misfit)
        data = data.reshape(BANDS, CX, CY, NZ, ELEMS).transpose(1, 0, 2, 3, 4).reshape(CX, NY, NZ, ELEMS)
        return (data - prior).astype(jnp.bfloat16).reshape(CX, NY, NZ * ELEMS)

    result = lax.map(final_block, jnp.arange(TILES, dtype=jnp.int32))
    return result.reshape(NX, NY, NZ * ELEMS)
```

```python
import functools

import jax
import jax.numpy as jnp
from jax import lax
from jax.experimental import pallas as pl
from jax.experimental.pallas import tpu as pltpu
from jax.sharding import PartitionSpec as P

BF = jnp.bfloat16
F32 = jnp.float32
MESH = pl.DeviceIdType.MESH
GROUP = 8


def dot(a, b):
    return jnp.dot(a, b, preferred_element_type=F32)


def dot_t(a, b):
    return lax.dot_general(a, b, (((1,), (1,)), ((), ())), preferred_element_type=F32)


def iota(shape, dim):
    return lax.broadcasted_iota(jnp.int32, shape, dim)


def put_wide(grid, row, values):
    for j in range(8):
        grid[j, row:row + values.shape[0], :] = values[:, j * 128:j * 128 + 128]


def put_column(grid, row, values):
    for j in range(8):
        grid[j, pl.ds(row, 8, stride=32), :] = values[:, j * 128:j * 128 + 128]


def get_column(grid, row):
    return jnp.concatenate([grid[j, pl.ds(row, 8, stride=32), :] for j in range(8)], axis=1)


def shifted(grid, jb, row, start, stop):
    return jnp.concatenate(
        [
            jnp.concatenate(
                [grid[2 * jb + k, x * 32 + row:x * 32 + row + 16, :] for x in range(start, stop)],
                axis=0,
            )
            for k in range(2)
        ],
        axis=1,
    )


def kernel(
    n, m,
    field, center, couple, index, counts, assays, weights,
    out,
    u, av, wv, iv, cv, kc, kd,
    stage, msg, got, code, gotcode,
    ysend, yrecv, csend, crecv,
    uf, uc, edge, imf, imx, wst, prior, rhs, acc, res,
    in_sem, out_sem, halo_send, halo_recv, list_send, list_recv, code_send, code_recv,
):
    gy, gx = lax.axis_index("gy"), lax.axis_index("gx")
    left, right = lax.rem(gx + n - 1, n), lax.rem(gx + 1, n)
    down, up = lax.rem(gy + m - 1, m), lax.rem(gy + 1, m)

    ins = [
        pltpu.make_async_copy(assays, av, in_sem.at[0]),
        pltpu.make_async_copy(weights, wv, in_sem.at[1]),
        pltpu.make_async_copy(field, u.at[pl.ds(2, 8)], in_sem.at[2]),
        pltpu.make_async_copy(index, iv, in_sem.at[3]),
        pltpu.make_async_copy(counts, cv, in_sem.at[4]),
        pltpu.make_async_copy(center, kc, in_sem.at[5]),
        pltpu.make_async_copy(couple, kd, in_sem.at[6]),
    ]
    for one in ins:
        one.start()

    barrier = pltpu.get_barrier_semaphore()

    def greet(d, _):
        pl.semaphore_signal(
            barrier, inc=1, device_id=(gy, lax.rem(gx + d, n)), device_id_type=MESH
        )
        return 0

    lax.fori_loop(1, n, greet, 0)
    for who in ((down, gx), (up, gx), (down, left), (down, right), (up, left), (up, right)):
        pl.semaphore_signal(barrier, inc=1, device_id=who, device_id_type=MESH)

    for which, (copy, src) in enumerate(((ins[0], av), (ins[1], wv))):
        copy.wait()
        for j in range(16):
            stage[pl.ds(j, n, stride=16), :] = src[:, j * 128:(j + 1) * 128].astype(F32)
        msg[:, which * 16:(which + 1) * 16, :] = stage[...].reshape(n, 16, 128).astype(BF)

    ins[3].wait()
    ins[4].wait()
    row, lane = iota((n, n), 0), iota((n, n), 1)
    count = jnp.sum(jnp.where(row == lane, cv[...].astype(F32), 0.0), axis=1, keepdims=True)
    used = iota((n, 32), 1).astype(F32) < count
    cells = jnp.where(used, iv[...], -1)
    pick_s, pick_l = iota((32, 128), 0), iota((32, 128), 1)
    pick = jnp.where(
        pick_s == 2 * lax.rem(pick_l, 16) + lax.rem(pick_l, 32) // 16, 1.0, 0.0
    ).astype(BF)
    high = dot(jnp.right_shift(cells, 4).astype(F32).astype(BF), pick)
    low = dot(jnp.bitwise_and(cells, 15).astype(F32).astype(BF), pick)
    codes = (high * 16.0 + low).astype(jnp.int32)
    for t in range(n):
        code[t] = codes[t:t + 1]

    ins[2].wait()
    for x in range(8):
        put_wide(uf, (x + 1) * 32 + 8, u[x + 2].astype(F32))

    def rows_at(y):
        return get_column(uf, 40 + y)

    ysend[0] = jnp.concatenate([rows_at(0), rows_at(1)], axis=0).astype(BF)
    ysend[1] = jnp.concatenate([rows_at(15), rows_at(14)], axis=0).astype(BF)
    for c, (x, y) in enumerate(((7, 15), (7, 0), (0, 15), (0, 0))):
        place = (x + 1) * 32 + 8 + y
        for j in range(8):
            csend[c, j:j + 1, :] = uf[j, place:place + 1, :]

    pl.semaphore_wait(barrier, n - 1 + 6)

    def remote(src, dst, send, recv, who):
        return pltpu.make_async_remote_copy(
            src_ref=src, dst_ref=dst, send_sem=send, recv_sem=recv,
            device_id=who, device_id_type=MESH,
        )

    halos = [
        remote(u.at[pl.ds(2, 2)], u.at[pl.ds(10, 2)], halo_send.at[0], halo_recv.at[0], (gy, left)),
        remote(u.at[pl.ds(8, 2)], u.at[pl.ds(0, 2)], halo_send.at[1], halo_recv.at[1], (gy, right)),
        remote(ysend.at[0], yrecv.at[1], halo_send.at[2], halo_recv.at[2], (down, gx)),
        remote(ysend.at[1], yrecv.at[0], halo_send.at[3], halo_recv.at[3], (up, gx)),
        remote(csend.at[0], crecv.at[0], halo_send.at[4], halo_recv.at[4], (up, right)),
        remote(csend.at[1], crecv.at[1], halo_send.at[5], halo_recv.at[5], (down, right)),
        remote(csend.at[2], crecv.at[2], halo_send.at[6], halo_recv.at[6], (up, left)),
        remote(csend.at[3], crecv.at[3], halo_send.at[7], halo_recv.at[7], (down, left)),
    ]
    for one in halos:
        one.start()

    def send_code(d, _):
        to = lax.rem(gx + d, n)
        remote(code.at[to], gotcode.at[d - 1], code_send.at[0], code_recv.at[0], (gy, to)).start()
        return 0

    lax.fori_loop(1, n, send_code, 0)

    def send_list(d, _):
        to = lax.rem(gx + d, n)
        remote(
            msg.at[to], got.at[d - 1], list_send.at[0], list_recv.at[(d - 1) // GROUP], (gy, to)
        ).start()
        return 0

    lax.fori_loop(1, n, send_list, 0)
    got[n - 1] = msg[gx]
    gotcode[n - 1] = code[gx]

    ins[5].wait()
    ins[6].wait()
    spread = jnp.where(lax.rem(iota((256, 64), 0), 64) == iota((256, 64), 1), 1.0, 0.0).astype(BF)
    rb, cb = iota((256, 256), 0) // 64, iota((256, 256), 1) // 64

    def tiled(block, flip):
        tall = (dot_t if flip else dot)(spread, block).astype(BF)
        return dot_t(tall, spread)

    for s in range(2):
        mid = tiled(kc[...], s == 1)
        above = tiled(kd[5 if s else 4], s == 1)
        below = tiled(kd[4 if s else 5], s == 1)
        for half in range(2):
            zr = rb - 2 + 4 * half
            window = jnp.where(zr == cb, mid, 0.0)
            window = jnp.where(zr == cb + 1, -above, window)
            window = jnp.where(zr == cb - 1, -below, window)
            wst[s, half * 256:half * 256 + 256, :] = window.astype(BF)
        for d in range(4):
            wst[s, 512 + d * 256:768 + d * 256, :] = jnp.where(
                rb == cb, -tiled(kd[d], s == 1), 0.0
            ).astype(BF)

    has_left, has_right, has_down, has_up = gx > 0, gx < n - 1, gy > 0, gy < m - 1
    for one in halos:
        one.wait_recv()
    zero = jnp.zeros((), F32)
    for slot, ok in ((0, has_left), (10, has_right)):
        for x in (slot, slot + 1):
            u[x] = jnp.where(ok, u[x].astype(F32), zero).astype(BF)
    put_wide(uf, 8, u[1].astype(F32))
    put_wide(uf, 9 * 32 + 8, u[10].astype(F32))
    low_y = jnp.where(has_down, yrecv[0].astype(F32), zero)
    high_y = jnp.where(has_up, yrecv[1].astype(F32), zero)
    put_column(uf, 32 + 7, low_y[0:8])
    put_column(uf, 32 + 24, high_y[0:8])
    for c, (x, y, ok) in enumerate(
        ((-1, -1, has_left & has_down), (-1, 16, has_left & has_up),
         (8, -1, has_right & has_down), (8, 16, has_right & has_up))
    ):
        place = (x + 1) * 32 + 8 + y
        for j in range(8):
            uf[j, place:place + 1, :] = jnp.where(ok, crecv[c, j:j + 1, :], zero)
    uc[:, 0:128] = jnp.zeros((160, 128), BF)
    uc[:, 1152:1280] = jnp.zeros((160, 128), BF)
    imx[:, 0:128] = jnp.zeros((160, 128), BF)
    imx[:, 1152:1280] = jnp.zeros((160, 128), BF)
    edge[:, :, 0:128] = jnp.zeros((5, 16, 128), BF)
    edge[:, :, 1152:1280] = jnp.zeros((5, 16, 128), BF)
    for x in range(10):
        uc[x * 16:x * 16 + 16, 128:1152] = u[x + 1]

    def pair(first, second):
        return jnp.concatenate([first, second], axis=0).astype(BF)

    edge[0, :, 128:1152] = pair(low_y[0:8], high_y[0:8])
    edge[1, :, 128:1152] = pair(get_column(uf, 64 + 7), get_column(uf, 64 + 24))
    edge[2, :, 128:1152] = pair(get_column(uf, 7), get_column(uf, 24))
    edge[3, :, 128:1152] = pair(rows_at(0), high_y[8:16])
    edge[4, :, 128:1152] = pair(low_y[8:16], rows_at(15))

    left_ok = jnp.where(has_left, 1.0, 0.0)
    right_ok = jnp.where(has_right, 1.0, 0.0)
    down_ok = jnp.where(has_down, 1.0, 0.0)
    up_ok = jnp.where(has_up, 1.0, 0.0)

    def image_part(jb, _):
        here = pl.ds(pl.multiple_of(jb * 256, 128), 256)
        inner = pl.ds(pl.multiple_of(jb * 256 + 128, 128), 256)
        window = pl.ds(pl.multiple_of(jb * 256, 128), 512)
        total = dot(uc[:, window], wst[0, 0:512])
        total += dot(u[2:12, :, here].reshape(160, 256), wst[0, 512:768])
        total += dot(u[0:10, :, here].reshape(160, 256), wst[0, 768:1024])
        plus = shifted(uf, jb, 9, 0, 10)
        total += dot(plus.astype(BF), wst[0, 1024:1280])
        minus = shifted(uf, jb, 7, 0, 10)
        total += dot(minus.astype(BF), wst[0, 1280:1536])
        rounded = total.astype(BF).astype(F32)
        for x in range(10):
            part = rounded[x * 16:x * 16 + 16]
            if x == 0:
                part = part * left_ok
            if x == 9:
                part = part * right_ok
            imx[x * 16:x * 16 + 16, inner] = part.astype(BF)
            for k in range(2):
                imf[2 * jb + k, x * 32 + 8:x * 32 + 24, :] = part[:, k * 128:k * 128 + 128]
        rim = dot(edge[0, :, window], wst[0, 0:512])
        for d in range(4):
            rim += dot(edge[d + 1, :, inner], wst[0, 512 + d * 256:768 + d * 256])
        rim = rim.astype(BF).astype(F32)
        for k in range(2):
            lanes = slice(k * 128, k * 128 + 128)
            imf[2 * jb + k, pl.ds(39, 8, stride=32), :] = rim[0:8, lanes] * down_ok
            imf[2 * jb + k, pl.ds(56, 8, stride=32), :] = rim[8:16, lanes] * up_ok
        return 0

    lax.fori_loop(0, 4, image_part, 0)

    def prior_part(jb, _):
        here = pl.ds(pl.multiple_of(jb * 256, 128), 256)
        inner = pl.ds(pl.multiple_of(jb * 256 + 128, 128), 256)
        window = pl.ds(pl.multiple_of(jb * 256, 128), 512)
        total = dot(imx[16:144, window], wst[1, 0:512])
        total += dot(imx[0:128, inner], wst[1, 512:768])
        total += dot(imx[32:160, inner], wst[1, 768:1024])
        minus = shifted(imf, jb, 7, 1, 9)
        total += dot(minus.astype(BF), wst[1, 1024:1280])
        plus = shifted(imf, jb, 9, 1, 9)
        total += dot(plus.astype(BF), wst[1, 1280:1536])
        prior[:, here] = total
        return 0

    lax.fori_loop(0, 4, prior_part, 0)

    some = gotcode.at[pl.ds(0, n - 1)]
    remote(some, some, code_send.at[0], code_recv.at[0], (gy, right)).wait_recv()
    low_lane = iota((GROUP * 16, 128), 1) < 64
    cell16 = iota((128, GROUP * 32), 0) * 16
    quarter = iota((1, 128), 1) // 32
    groups = n // GROUP
    for g in range(groups):
        first = g * GROUP
        arriving = GROUP if g < groups - 1 else GROUP - 1
        part = got.at[pl.ds(first, arriving)]
        remote(part, part, list_send.at[0], list_recv.at[g], (gy, right)).wait_recv()
        a = got[first:first + GROUP, 0:16, :].astype(F32).reshape(GROUP * 16, 128)
        w = got[first:first + GROUP, 16:32, :].astype(F32).reshape(GROUP * 16, 128)
        p = a * w
        hi = p.astype(BF).astype(F32)
        lo = p - hi
        wr, hir, lor = (pltpu.roll(v, 64, 1) for v in (w, hi, lo))
        for parity, slots, one, two in (
            (0, 0, jnp.where(low_lane, hi, wr), lo),
            (0, 1, jnp.where(low_lane, hir, w), lor),
            (1, 0, jnp.where(low_lane, w, hir), lor),
            (1, 1, jnp.where(low_lane, wr, hi), lo),
        ):
            at = slice(slots * 16, slots * 16 + 16)
            rhs[parity, :, at, 0:128] = one.astype(BF).reshape(GROUP, 16, 128)
            rhs[parity, :, at, 128:256] = two.astype(BF).reshape(GROUP, 16, 128)
        keys = []
        for q in range(GROUP // 4):
            key = gotcode[first + 4 * q]
            for o in range(1, 4):
                key = jnp.where(quarter == o, gotcode[first + 4 * q + o], key)
            keys.append(key)
        key = jnp.concatenate(keys, axis=1)

        def layer(zz, _, g=g, key=key):
            for parity in range(2):
                z = 2 * zz + parity
                hit = jnp.where(cell16 == key - z, 1.0, 0.0).astype(BF)
                part = dot(hit, rhs[parity].reshape(GROUP * 32, 256))
                acc[z] = part if g == 0 else acc[z] + part
            return 0

        lax.fori_loop(0, 8, layer, 0)

    low_out = iota((128, 128), 1) < 64
    for zz in range(8):
        even, odd = acc[2 * zz], acc[2 * zz + 1]
        lanes = slice(zz * 128, zz * 128 + 128)
        s1 = jnp.where(low_out, even[:, 0:128] + even[:, 128:256], odd[:, 0:128] + odd[:, 128:256])
        s0 = pltpu.roll(jnp.where(low_out, odd[:, 0:128], even[:, 0:128]), 64, 1)
        own = u[2:10, :, lanes].astype(F32).reshape(128, 128)
        grad = s1 - own * s0 - prior[:, lanes]
        res[:, :, lanes] = grad.astype(BF).reshape(8, 16, 128)

    put = pltpu.make_async_copy(res, out, out_sem.at[0])
    put.start()
    for one in halos:
        one.wait_send()
    remote(some, some, code_send.at[0], code_recv.at[0], (gy, right)).wait_send()
    every = got.at[pl.ds(0, n - 1)]
    remote(every, every, list_send.at[0], list_recv.at[0], (gy, right)).wait_send()
    put.wait()


def on_device(field, center_block, couple_blocks, cell_index, slot_counts, assays, assay_weights):
    n, m = lax.axis_size("gx"), lax.axis_size("gy")
    vm, dma = pltpu.VMEM, pltpu.SemaphoreType.DMA
    i32 = jnp.int32
    return pl.pallas_call(
        functools.partial(kernel, n, m),
        out_shape=jax.ShapeDtypeStruct(field.shape, BF),
        in_specs=[pl.BlockSpec(memory_space=pl.ANY)] * 7,
        out_specs=pl.BlockSpec(memory_space=pl.ANY),
        scratch_shapes=[
            vm((12, 16, 1024), BF),
            vm((n, 2048), BF),
            vm((n, 2048), BF),
            vm((n, 32), i32),
            vm((1, n), i32),
            vm((64, 64), BF),
            vm((6, 64, 64), BF),
            vm((n * 16, 128), F32),
            vm((n, 32, 128), BF),
            vm((n, 32, 128), BF),
            vm((n, 1, 128), i32),
            vm((n, 1, 128), i32),
            vm((2, 16, 1024), BF),
            vm((2, 16, 1024), BF),
            vm((4, 8, 128), F32),
            vm((4, 8, 128), F32),
            vm((8, 320, 128), F32),
            vm((160, 1280), BF),
            vm((5, 16, 1280), BF),
            vm((8, 320, 128), F32),
            vm((160, 1280), BF),
            vm((2, 1536, 256), BF),
            vm((128, 1024), F32),
            vm((2, GROUP, 32, 256), BF),
            vm((16, 128, 256), F32),
            vm((8, 16, 1024), BF),
            dma((7,)), dma((1,)), dma((8,)), dma((8,)),
            dma((1,)), dma((n // GROUP,)), dma((1,)), dma((1,)),
        ],
        compiler_params=pltpu.CompilerParams(
            collective_id=0, has_side_effects=True, vmem_limit_bytes=40 * 1024 * 1024
        ),
    )(
        field, center_block, couple_blocks, cell_index.reshape(n, 32),
        slot_counts.reshape(1, n), assays.reshape(n, 2048), assay_weights.reshape(n, 2048),
    )


def solution(mesh):
    in_specs = (
        P("gx", "gy", None),
        P(),
        P(),
        P("gy", "gx", None, None),
        P("gy", "gx", None),
        P("gy", "gx", None, None),
        P("gy", "gx", None, None),
    )
    return jax.shard_map(
        on_device, mesh=mesh, in_specs=in_specs, out_specs=P("gx", "gy", None), check_vma=False
    )
```

```python
import functools

import jax
import jax.numpy as jnp
from jax import lax
from jax.experimental import pallas as pl
from jax.experimental.pallas import tpu as pltpu
from jax.sharding import PartitionSpec as P

BF = jnp.bfloat16
F32 = jnp.float32
MESH = pl.DeviceIdType.MESH
GROUP = 8


def dot(a, b):
    return jnp.dot(a, b, preferred_element_type=F32)


def dot_t(a, b):
    return lax.dot_general(a, b, (((1,), (1,)), ((), ())), preferred_element_type=F32)


def iota(shape, dim):
    return lax.broadcasted_iota(jnp.int32, shape, dim)


def put_wide(grid, row, values):
    for j in range(8):
        grid[j, row:row + values.shape[0], :] = values[:, j * 128:j * 128 + 128]


def put_column(grid, row, values):
    for j in range(8):
        grid[j, pl.ds(row, 8, stride=32), :] = values[:, j * 128:j * 128 + 128]


def get_column(grid, row):
    return jnp.concatenate([grid[j, pl.ds(row, 8, stride=32), :] for j in range(8)], axis=1)


def shifted(grid, jb, row, start, stop):
    return jnp.concatenate(
        [
            jnp.concatenate(
                [grid[2 * jb + k, x * 32 + row:x * 32 + row + 16, :] for x in range(start, stop)],
                axis=0,
            )
            for k in range(2)
        ],
        axis=1,
    )


def kernel(
    n, m,
    field, center, couple, index, counts, assays, weights,
    out,
    u, av, wv, iv, cv, kc, kd,
    stage, msg, got, code, gotcode,
    ysend, yrecv, csend, crecv,
    uf, uc, edge, imf, imx, wst, prior, rhs, hot, acc, res,
    in_sem, out_sem, halo_send, halo_recv, list_send, list_recv, code_send, code_recv,
):
    gy, gx = lax.axis_index("gy"), lax.axis_index("gx")
    left, right = lax.rem(gx + n - 1, n), lax.rem(gx + 1, n)
    down, up = lax.rem(gy + m - 1, m), lax.rem(gy + 1, m)

    ins = [
        pltpu.make_async_copy(assays, av, in_sem.at[0]),
        pltpu.make_async_copy(weights, wv, in_sem.at[1]),
        pltpu.make_async_copy(field, u.at[pl.ds(2, 8)], in_sem.at[2]),
        pltpu.make_async_copy(index, iv, in_sem.at[3]),
        pltpu.make_async_copy(counts, cv, in_sem.at[4]),
        pltpu.make_async_copy(center, kc, in_sem.at[5]),
        pltpu.make_async_copy(couple, kd, in_sem.at[6]),
    ]
    for one in ins:
        one.start()

    barrier = pltpu.get_barrier_semaphore()

    def greet(d, _):
        pl.semaphore_signal(
            barrier, inc=1, device_id=(gy, lax.rem(gx + d, n)), device_id_type=MESH
        )
        return 0

    lax.fori_loop(1, n, greet, 0)
    for who in ((down, gx), (up, gx), (down, left), (down, right), (up, left), (up, right)):
        pl.semaphore_signal(barrier, inc=1, device_id=who, device_id_type=MESH)

    for which, (copy, src) in enumerate(((ins[0], av), (ins[1], wv))):
        copy.wait()
        for j in range(16):
            stage[pl.ds(j, n, stride=16), :] = src[:, j * 128:(j + 1) * 128].astype(F32)
        msg[:, which * 16:(which + 1) * 16, :] = stage[...].reshape(n, 16, 128).astype(BF)

    ins[3].wait()
    ins[4].wait()
    row, lane = iota((n, n), 0), iota((n, n), 1)
    count = jnp.sum(jnp.where(row == lane, cv[...].astype(F32), 0.0), axis=1, keepdims=True)
    used = iota((n, 32), 1).astype(F32) < count
    cells = jnp.where(used, iv[...], -1)
    pick_s, pick_l = iota((32, 128), 0), iota((32, 128), 1)
    pick = jnp.where(
        pick_s == 2 * lax.rem(pick_l, 16) + lax.rem(pick_l, 32) // 16, 1.0, 0.0
    ).astype(BF)
    high = dot(jnp.right_shift(cells, 4).astype(F32).astype(BF), pick)
    low = dot(jnp.bitwise_and(cells, 15).astype(F32).astype(BF), pick)
    codes = (high * 16.0 + low).astype(jnp.int32)
    for t in range(n):
        code[t] = codes[t:t + 1]

    ins[2].wait()
    for x in range(8):
        put_wide(uf, (x + 1) * 32 + 8, u[x + 2].astype(F32))

    def rows_at(y):
        return get_column(uf, 40 + y)

    ysend[0] = jnp.concatenate([rows_at(0), rows_at(1)], axis=0).astype(BF)
    ysend[1] = jnp.concatenate([rows_at(15), rows_at(14)], axis=0).astype(BF)
    for c, (x, y) in enumerate(((7, 15), (7, 0), (0, 15), (0, 0))):
        place = (x + 1) * 32 + 8 + y
        for j in range(8):
            csend[c, j:j + 1, :] = uf[j, place:place + 1, :]

    pl.semaphore_wait(barrier, n - 1 + 6)

    def remote(src, dst, send, recv, who):
        return pltpu.make_async_remote_copy(
            src_ref=src, dst_ref=dst, send_sem=send, recv_sem=recv,
            device_id=who, device_id_type=MESH,
        )

    halos = [
        remote(u.at[pl.ds(2, 2)], u.at[pl.ds(10, 2)], halo_send.at[0], halo_recv.at[0], (gy, left)),
        remote(u.at[pl.ds(8, 2)], u.at[pl.ds(0, 2)], halo_send.at[1], halo_recv.at[1], (gy, right)),
        remote(ysend.at[0], yrecv.at[1], halo_send.at[2], halo_recv.at[2], (down, gx)),
        remote(ysend.at[1], yrecv.at[0], halo_send.at[3], halo_recv.at[3], (up, gx)),
        remote(csend.at[0], crecv.at[0], halo_send.at[4], halo_recv.at[4], (up, right)),
        remote(csend.at[1], crecv.at[1], halo_send.at[5], halo_recv.at[5], (down, right)),
        remote(csend.at[2], crecv.at[2], halo_send.at[6], halo_recv.at[6], (up, left)),
        remote(csend.at[3], crecv.at[3], halo_send.at[7], halo_recv.at[7], (down, left)),
    ]
    for one in halos:
        one.start()

    def send_code(d, _):
        to = lax.rem(gx + d, n)
        remote(code.at[to], gotcode.at[d - 1], code_send.at[0], code_recv.at[0], (gy, to)).start()
        return 0

    lax.fori_loop(1, n, send_code, 0)

    def send_list(d, _):
        to = lax.rem(gx + d, n)
        remote(
            msg.at[to], got.at[d - 1], list_send.at[0], list_recv.at[(d - 1) // GROUP], (gy, to)
        ).start()
        return 0

    lax.fori_loop(1, n, send_list, 0)
    got[n - 1] = msg[gx]
    gotcode[n - 1] = code[gx]

    def matrices():
        ins[5].wait()
        ins[6].wait()
        spread = jnp.where(lax.rem(iota((256, 64), 0), 64) == iota((256, 64), 1), 1.0, 0.0).astype(BF)
        rb, cb = iota((256, 256), 0) // 64, iota((256, 256), 1) // 64

        def tiled(block, flip):
            tall = (dot_t if flip else dot)(spread, block).astype(BF)
            return dot_t(tall, spread)

        for s in range(2):
            mid = tiled(kc[...], s == 1)
            above = tiled(kd[5 if s else 4], s == 1)
            below = tiled(kd[4 if s else 5], s == 1)
            for half in range(2):
                zr = rb - 2 + 4 * half
                window = jnp.where(zr == cb, mid, 0.0)
                window = jnp.where(zr == cb + 1, -above, window)
                window = jnp.where(zr == cb - 1, -below, window)
                wst[s, half * 256:half * 256 + 256, :] = window.astype(BF)
            for d in range(4):
                wst[s, 512 + d * 256:768 + d * 256, :] = jnp.where(
                    rb == cb, -tiled(kd[d], s == 1), 0.0
                ).astype(BF)

    def beyond():
        has_left, has_right, has_down, has_up = gx > 0, gx < n - 1, gy > 0, gy < m - 1
        for one in halos:
            one.wait_recv()
        zero = jnp.zeros((), F32)
        for slot, ok in ((0, has_left), (10, has_right)):
            for x in (slot, slot + 1):
                u[x] = jnp.where(ok, u[x].astype(F32), zero).astype(BF)
        put_wide(uf, 8, u[1].astype(F32))
        put_wide(uf, 9 * 32 + 8, u[10].astype(F32))
        low_y = jnp.where(has_down, yrecv[0].astype(F32), zero)
        high_y = jnp.where(has_up, yrecv[1].astype(F32), zero)
        put_column(uf, 32 + 7, low_y[0:8])
        put_column(uf, 32 + 24, high_y[0:8])
        for c, (x, y, ok) in enumerate(
            ((-1, -1, has_left & has_down), (-1, 16, has_left & has_up),
             (8, -1, has_right & has_down), (8, 16, has_right & has_up))
        ):
            place = (x + 1) * 32 + 8 + y
            for j in range(8):
                uf[j, place:place + 1, :] = jnp.where(ok, crecv[c, j:j + 1, :], zero)
        uc[:, 0:128] = jnp.zeros((160, 128), BF)
        uc[:, 1152:1280] = jnp.zeros((160, 128), BF)
        imx[:, 0:128] = jnp.zeros((160, 128), BF)
        imx[:, 1152:1280] = jnp.zeros((160, 128), BF)
        edge[:, :, 0:128] = jnp.zeros((5, 16, 128), BF)
        edge[:, :, 1152:1280] = jnp.zeros((5, 16, 128), BF)
        for x in range(10):
            uc[x * 16:x * 16 + 16, 128:1152] = u[x + 1]

        def pair(first, second):
            return jnp.concatenate([first, second], axis=0).astype(BF)

        edge[0, :, 128:1152] = pair(low_y[0:8], high_y[0:8])
        edge[1, :, 128:1152] = pair(get_column(uf, 64 + 7), get_column(uf, 64 + 24))
        edge[2, :, 128:1152] = pair(get_column(uf, 7), get_column(uf, 24))
        edge[3, :, 128:1152] = pair(rows_at(0), high_y[8:16])
        edge[4, :, 128:1152] = pair(low_y[8:16], rows_at(15))

        left_ok = jnp.where(has_left, 1.0, 0.0)
        right_ok = jnp.where(has_right, 1.0, 0.0)
        down_ok = jnp.where(has_down, 1.0, 0.0)
        up_ok = jnp.where(has_up, 1.0, 0.0)

        def image_part(jb, _):
            here = pl.ds(pl.multiple_of(jb * 256, 128), 256)
            inner = pl.ds(pl.multiple_of(jb * 256 + 128, 128), 256)
            window = pl.ds(pl.multiple_of(jb * 256, 128), 512)
            total = dot(uc[:, window], wst[0, 0:512])
            total += dot(u[2:12, :, here].reshape(160, 256), wst[0, 512:768])
            total += dot(u[0:10, :, here].reshape(160, 256), wst[0, 768:1024])
            plus = shifted(uf, jb, 9, 0, 10)
            total += dot(plus.astype(BF), wst[0, 1024:1280])
            minus = shifted(uf, jb, 7, 0, 10)
            total += dot(minus.astype(BF), wst[0, 1280:1536])
            rounded = total.astype(BF).astype(F32)
            for x in range(10):
                part = rounded[x * 16:x * 16 + 16]
                if x == 0:
                    part = part * left_ok
                if x == 9:
                    part = part * right_ok
                imx[x * 16:x * 16 + 16, inner] = part.astype(BF)
                for k in range(2):
                    imf[2 * jb + k, x * 32 + 8:x * 32 + 24, :] = part[:, k * 128:k * 128 + 128]
            rim = dot(edge[0, :, window], wst[0, 0:512])
            for d in range(4):
                rim += dot(edge[d + 1, :, inner], wst[0, 512 + d * 256:768 + d * 256])
            rim = rim.astype(BF).astype(F32)
            for k in range(2):
                lanes = slice(k * 128, k * 128 + 128)
                imf[2 * jb + k, pl.ds(39, 8, stride=32), :] = rim[0:8, lanes] * down_ok
                imf[2 * jb + k, pl.ds(56, 8, stride=32), :] = rim[8:16, lanes] * up_ok
            return 0

        lax.fori_loop(0, 4, image_part, 0)

        def prior_part(jb, _):
            here = pl.ds(pl.multiple_of(jb * 256, 128), 256)
            inner = pl.ds(pl.multiple_of(jb * 256 + 128, 128), 256)
            window = pl.ds(pl.multiple_of(jb * 256, 128), 512)
            total = dot(imx[16:144, window], wst[1, 0:512])
            total += dot(imx[0:128, inner], wst[1, 512:768])
            total += dot(imx[32:160, inner], wst[1, 768:1024])
            minus = shifted(imf, jb, 7, 1, 9)
            total += dot(minus.astype(BF), wst[1, 1024:1280])
            plus = shifted(imf, jb, 9, 1, 9)
            total += dot(plus.astype(BF), wst[1, 1280:1536])
            prior[:, here] = total
            return 0

        lax.fori_loop(0, 4, prior_part, 0)

    def codes_in():
        remote(some, some, code_send.at[0], code_recv.at[0], (gy, right)).wait_recv()
        quarter = iota((1, 128), 1) // 32
        rows128 = iota((128, 128), 0)

        def hits(q, _):
            key = gotcode[4 * q]
            for o in range(1, 4):
                key = jnp.where(quarter == o, gotcode[4 * q + o], key)
            hit = jnp.where(rows128 == jnp.right_shift(key, 4), 1.0, 0.0).astype(BF).reshape(8, 16, 128)
            layer = jnp.broadcast_to(jnp.bitwise_and(key, 15), (16, 128))
            lanes = pl.ds(pl.multiple_of(q * 128, 128), 128)
            for z in range(16):
                only = jnp.where(layer == z, 1.0, 0.0).astype(BF)
                hot[z % 2, z // 2 * 128:z // 2 * 128 + 128, lanes] = (hit * only).reshape(128, 128)
            return 0

        lax.fori_loop(0, n // 4, hits, 0)

    low_lane = iota((GROUP * 16, 128), 1) < 64
    groups = n // GROUP

    def take(g):
        first = g * GROUP
        arriving = GROUP if g < groups - 1 else GROUP - 1
        part = got.at[pl.ds(first, arriving)]
        remote(part, part, list_send.at[0], list_recv.at[g], (gy, right)).wait_recv()
        a = got[first:first + GROUP, 0:16, :].astype(F32).reshape(GROUP * 16, 128)
        w = got[first:first + GROUP, 16:32, :].astype(F32).reshape(GROUP * 16, 128)
        p = a * w
        hi = p.astype(BF).astype(F32)
        lo = p - hi
        wr, hir, lor = (pltpu.roll(v, 64, 1) for v in (w, hi, lo))
        for parity, slots, one, two in (
            (0, 0, jnp.where(low_lane, hi, wr), lo),
            (0, 1, jnp.where(low_lane, hir, w), lor),
            (1, 0, jnp.where(low_lane, w, hir), lor),
            (1, 1, jnp.where(low_lane, wr, hi), lo),
        ):
            at = slice(slots * 16, slots * 16 + 16)
            rhs[parity, first:first + GROUP, at, 0:128] = one.astype(BF).reshape(GROUP, 16, 128)
            rhs[parity, first:first + GROUP, at, 128:256] = two.astype(BF).reshape(GROUP, 16, 128)

    def add(start, stop):
        for parity in range(2):
            lists = rhs[parity, start * GROUP:stop * GROUP].reshape(-1, 256)
            part = dot(hot[parity, :, start * GROUP * 32:stop * GROUP * 32], lists)
            acc[parity] = part if start == 0 else acc[parity] + part

    some = gotcode.at[pl.ds(0, n - 1)]
    matrices()
    codes_in()
    take(0)
    beyond()
    for g in range(1, groups - 1):
        take(g)
    add(0, groups - 1)
    take(groups - 1)
    add(groups - 1, groups)

    low_out = iota((128, 128), 1) < 64
    for zz in range(8):
        rows = slice(zz * 128, zz * 128 + 128)
        even, odd = acc[0, rows], acc[1, rows]
        s1 = jnp.where(low_out, even[:, 0:128] + even[:, 128:256], odd[:, 0:128] + odd[:, 128:256])
        s0 = pltpu.roll(jnp.where(low_out, odd[:, 0:128], even[:, 0:128]), 64, 1)
        own = u[2:10, :, rows].astype(F32).reshape(128, 128)
        grad = s1 - own * s0 - prior[:, rows]
        res[:, :, rows] = grad.astype(BF).reshape(8, 16, 128)

    put = pltpu.make_async_copy(res, out, out_sem.at[0])
    put.start()
    for one in halos:
        one.wait_send()
    remote(some, some, code_send.at[0], code_recv.at[0], (gy, right)).wait_send()
    every = got.at[pl.ds(0, n - 1)]
    remote(every, every, list_send.at[0], list_recv.at[0], (gy, right)).wait_send()
    put.wait()


def on_device(field, center_block, couple_blocks, cell_index, slot_counts, assays, assay_weights):
    n, m = lax.axis_size("gx"), lax.axis_size("gy")
    vm, dma = pltpu.VMEM, pltpu.SemaphoreType.DMA
    i32 = jnp.int32
    return pl.pallas_call(
        functools.partial(kernel, n, m),
        out_shape=jax.ShapeDtypeStruct(field.shape, BF),
        in_specs=[pl.BlockSpec(memory_space=pltpu.HBM)] * 7,
        out_specs=pl.BlockSpec(memory_space=pltpu.HBM),
        scratch_shapes=[
            vm((12, 16, 1024), BF),
            vm((n, 2048), BF),
            vm((n, 2048), BF),
            vm((n, 32), i32),
            vm((1, n), i32),
            vm((64, 64), BF),
            vm((6, 64, 64), BF),
            vm((n * 16, 128), F32),
            vm((n, 32, 128), BF),
            vm((n, 32, 128), BF),
            vm((n, 1, 128), i32),
            vm((n, 1, 128), i32),
            vm((2, 16, 1024), BF),
            vm((2, 16, 1024), BF),
            vm((4, 8, 128), F32),
            vm((4, 8, 128), F32),
            vm((8, 320, 128), F32),
            vm((160, 1280), BF),
            vm((5, 16, 1280), BF),
            vm((8, 320, 128), F32),
            vm((160, 1280), BF),
            vm((2, 1536, 256), BF),
            vm((128, 1024), F32),
            vm((2, n, 32, 256), BF),
            vm((2, 1024, n * 32), BF),
            vm((2, 1024, 256), F32),
            vm((8, 16, 1024), BF),
            dma((7,)), dma((1,)), dma((8,)), dma((8,)),
            dma((1,)), dma((n // GROUP,)), dma((1,)), dma((1,)),
        ],
        compiler_params=pltpu.CompilerParams(
            collective_id=0, has_side_effects=True, vmem_limit_bytes=56 * 1024 * 1024
        ),
    )(
        field, center_block, couple_blocks, cell_index.reshape(n, 32),
        slot_counts.reshape(1, n), assays.reshape(n, 2048), assay_weights.reshape(n, 2048),
    )


def solution(mesh):
    in_specs = (
        P("gx", "gy", None),
        P(),
        P(),
        P("gy", "gx", None, None),
        P("gy", "gx", None),
        P("gy", "gx", None, None),
        P("gy", "gx", None, None),
    )
    return jax.shard_map(
        on_device, mesh=mesh, in_specs=in_specs, out_specs=P("gx", "gy", None), check_vma=False
    )
```

```python
import functools

import jax
import jax.numpy as jnp
from jax import lax
from jax.experimental import pallas as pl
from jax.experimental.pallas import tpu as pltpu
from jax.sharding import PartitionSpec as P

BF = jnp.bfloat16
F32 = jnp.float32
MESH = pl.DeviceIdType.MESH
SENT = (0, 1, 3, 2)
ZS = 4


def dot(a, b):
    return jnp.dot(a, b, preferred_element_type=F32)


def dot_t(a, b):
    return lax.dot_general(a, b, (((1,), (1,)), ((), ())), preferred_element_type=F32)


def iota(shape, dim):
    return lax.broadcasted_iota(jnp.int32, shape, dim)


def put_wide(grid, row, values):
    for j in range(8):
        grid[j, row:row + values.shape[0], :] = values[:, j * 128:j * 128 + 128]


def put_column(grid, row, values):
    for j in range(8):
        grid[j, pl.ds(row, 8, stride=32), :] = values[:, j * 128:j * 128 + 128]


def get_column(grid, row):
    return jnp.concatenate([grid[j, pl.ds(row, 8, stride=32), :] for j in range(8)], axis=1)


def shifted(grid, jb, row, start, stop):
    return jnp.concatenate(
        [
            jnp.concatenate(
                [grid[2 * jb + k, x * 32 + row:x * 32 + row + 16, :] for x in range(start, stop)],
                axis=0,
            )
            for k in range(2)
        ],
        axis=1,
    )


def kernel(
    n, m,
    field, center, couple, index, counts, assays, weights,
    out,
    u, av, wv, iv, cv, kc, kd,
    stage, msg, got, code, gotcode,
    ysend, yrecv, csend, crecv,
    uf, uc, edge, imf, imx, wst, prior, rhs, hot, acc, res,
    in_sem, out_sem, halo_send, halo_recv, list_send, list_recv, code_send, code_recv,
):
    gy, gx = lax.axis_index("gy"), lax.axis_index("gx")
    left, right = lax.rem(gx + n - 1, n), lax.rem(gx + 1, n)
    down, up = lax.rem(gy + m - 1, m), lax.rem(gy + 1, m)

    ins = [
        pltpu.make_async_copy(assays, av, in_sem.at[0]),
        pltpu.make_async_copy(weights, wv, in_sem.at[1]),
        pltpu.make_async_copy(field, u.at[pl.ds(2, 8)], in_sem.at[2]),
        pltpu.make_async_copy(index, iv, in_sem.at[3]),
        pltpu.make_async_copy(counts, cv, in_sem.at[4]),
        pltpu.make_async_copy(center, kc, in_sem.at[5]),
        pltpu.make_async_copy(couple, kd, in_sem.at[6]),
    ]
    for one in ins:
        one.start()

    size = n // ZS
    barrier = pltpu.get_barrier_semaphore()

    def greet(d, _):
        pl.semaphore_signal(
            barrier, inc=1, device_id=(gy, lax.rem(gx + d, n)), device_id_type=MESH
        )
        return 0

    lax.fori_loop(1, n, greet, 0)
    has_left, has_right, has_down, has_up = gx > 0, gx < n - 1, gy > 0, gy < m - 1
    beside = (
        (has_down, (down, gx)), (has_up, (up, gx)),
        (has_down & has_left, (down, left)), (has_down & has_right, (down, right)),
        (has_up & has_left, (up, left)), (has_up & has_right, (up, right)),
    )
    greetings = n - 1
    for there, who in beside:
        greetings += jnp.where(there, 1, 0)

        @pl.when(there)
        def _(who=who):
            pl.semaphore_signal(barrier, inc=1, device_id=who, device_id_type=MESH)

    for which, (copy, src) in enumerate(((ins[0], av), (ins[1], wv))):
        copy.wait()
        for j in range(16):
            stage[pl.ds(j, n, stride=16), :] = src[:, j * 128:(j + 1) * 128].astype(F32)
        msg[:, which * 16:(which + 1) * 16, :] = stage[...].reshape(n, 16, 128).astype(BF)

    ins[3].wait()
    ins[4].wait()
    row, lane = iota((n, n), 0), iota((n, n), 1)
    count = jnp.sum(jnp.where(row == lane, cv[...].astype(F32), 0.0), axis=1, keepdims=True)
    used = iota((n, 32), 1).astype(F32) < count
    cells = jnp.where(used, iv[...], -1)
    pick_s, pick_l = iota((32, 128), 0), iota((32, 128), 1)
    pick = jnp.where(
        pick_s == 2 * lax.rem(pick_l, 16) + lax.rem(pick_l, 32) // 16, 1.0, 0.0
    ).astype(BF)
    high = dot(jnp.right_shift(cells, 4).astype(F32).astype(BF), pick)
    low = dot(jnp.bitwise_and(cells, 15).astype(F32).astype(BF), pick)
    codes = (high * 16.0 + low).astype(jnp.int32)
    for t in range(n):
        code[t] = codes[t:t + 1]

    ins[2].wait()
    for x in range(8):
        put_wide(uf, (x + 1) * 32 + 8, u[x + 2].astype(F32))

    def rows_at(y):
        return get_column(uf, 40 + y)

    ysend[0] = jnp.concatenate([rows_at(0), rows_at(1)], axis=0).astype(BF)
    ysend[1] = jnp.concatenate([rows_at(15), rows_at(14)], axis=0).astype(BF)
    for c, (x, y) in enumerate(((7, 15), (7, 0), (0, 15), (0, 0))):
        place = (x + 1) * 32 + 8 + y
        for j in range(8):
            csend[c, j:j + 1, :] = uf[j, place:place + 1, :]

    pl.semaphore_wait(barrier, greetings)

    def remote(src, dst, send, recv, who):
        return pltpu.make_async_remote_copy(
            src_ref=src, dst_ref=dst, send_sem=send, recv_sem=recv,
            device_id=who, device_id_type=MESH,
        )

    halos = [
        (has_left, has_right, u.at[pl.ds(2, 2)], u.at[pl.ds(10, 2)], (gy, left)),
        (has_right, has_left, u.at[pl.ds(8, 2)], u.at[pl.ds(0, 2)], (gy, right)),
        (has_down, has_up, ysend.at[0], yrecv.at[1], (down, gx)),
        (has_up, has_down, ysend.at[1], yrecv.at[0], (up, gx)),
        (has_up & has_right, has_down & has_left, csend.at[0], crecv.at[0], (up, right)),
        (has_down & has_right, has_up & has_left, csend.at[1], crecv.at[1], (down, right)),
        (has_up & has_left, has_down & has_right, csend.at[2], crecv.at[2], (up, left)),
        (has_down & has_left, has_up & has_right, csend.at[3], crecv.at[3], (down, left)),
    ]

    def halo(k, what):
        sends, receives, src, dst, who = halos[k]
        copy = remote(src, dst, halo_send.at[k], halo_recv.at[k], who)

        @pl.when(receives if what == "wait_recv" else sends)
        def _():
            getattr(copy, what)()

    for k in range(8):
        halo(k, "start")

    def partner(g, k):
        y, z, c = gx // 8 + k // 2, lax.rem(gx // 2, ZS) + g, lax.rem(gx, 2) + lax.rem(k, 2)
        return lax.rem(y, n // 8) * 8 + lax.rem(z, ZS) * 2 + lax.rem(c, 2)

    def send_code(g, k):
        to = partner(g, k)
        remote(code.at[to], gotcode.at[g * size + k], code_send.at[0], code_recv.at[0], (gy, to)).start()

    def send_list(g, k):
        to = partner(g, k)
        remote(msg.at[to], got.at[g * size + k], list_send.at[0], list_recv.at[g], (gy, to)).start()

    for send in (send_code, send_list):
        for g in SENT:

            def each(k, _, g=g, send=send):
                send(g, k)
                return 0

            lax.fori_loop(1 if g == 0 else 0, size, each, 0)
    got[0] = msg[gx]
    gotcode[0] = code[gx]

    def matrices():
        ins[5].wait()
        ins[6].wait()
        spread = jnp.where(lax.rem(iota((256, 64), 0), 64) == iota((256, 64), 1), 1.0, 0.0).astype(BF)
        rb, cb = iota((256, 256), 0) // 64, iota((256, 256), 1) // 64

        def tiled(block, flip):
            tall = (dot_t if flip else dot)(spread, block).astype(BF)
            return dot_t(tall, spread)

        for s in range(2):
            mid = tiled(kc[...], s == 1)
            above = tiled(kd[5 if s else 4], s == 1)
            below = tiled(kd[4 if s else 5], s == 1)
            for half in range(2):
                zr = rb - 2 + 4 * half
                window = jnp.where(zr == cb, mid, 0.0)
                window = jnp.where(zr == cb + 1, -above, window)
                window = jnp.where(zr == cb - 1, -below, window)
                wst[s, half * 256:half * 256 + 256, :] = window.astype(BF)
            for d in range(4):
                wst[s, 512 + d * 256:768 + d * 256, :] = jnp.where(
                    rb == cb, -tiled(kd[d], s == 1), 0.0
                ).astype(BF)

    def beyond():
        for k in range(8):
            halo(k, "wait_recv")
        zero = jnp.zeros((), F32)
        for slot, ok in ((0, has_left), (10, has_right)):
            for x in (slot, slot + 1):
                u[x] = jnp.where(ok, u[x].astype(F32), zero).astype(BF)
        put_wide(uf, 8, u[1].astype(F32))
        put_wide(uf, 9 * 32 + 8, u[10].astype(F32))
        low_y = jnp.where(has_down, yrecv[0].astype(F32), zero)
        high_y = jnp.where(has_up, yrecv[1].astype(F32), zero)
        put_column(uf, 32 + 7, low_y[0:8])
        put_column(uf, 32 + 24, high_y[0:8])
        for c, (x, y, ok) in enumerate(
            ((-1, -1, has_left & has_down), (-1, 16, has_left & has_up),
             (8, -1, has_right & has_down), (8, 16, has_right & has_up))
        ):
            place = (x + 1) * 32 + 8 + y
            for j in range(8):
                uf[j, place:place + 1, :] = jnp.where(ok, crecv[c, j:j + 1, :], zero)
        uc[:, 0:128] = jnp.zeros((160, 128), BF)
        uc[:, 1152:1280] = jnp.zeros((160, 128), BF)
        imx[:, 0:128] = jnp.zeros((160, 128), BF)
        imx[:, 1152:1280] = jnp.zeros((160, 128), BF)
        edge[:, :, 0:128] = jnp.zeros((5, 16, 128), BF)
        edge[:, :, 1152:1280] = jnp.zeros((5, 16, 128), BF)
        for x in range(10):
            uc[x * 16:x * 16 + 16, 128:1152] = u[x + 1]

        def pair(first, second):
            return jnp.concatenate([first, second], axis=0).astype(BF)

        edge[0, :, 128:1152] = pair(low_y[0:8], high_y[0:8])
        edge[1, :, 128:1152] = pair(get_column(uf, 64 + 7), get_column(uf, 64 + 24))
        edge[2, :, 128:1152] = pair(get_column(uf, 7), get_column(uf, 24))
        edge[3, :, 128:1152] = pair(rows_at(0), high_y[8:16])
        edge[4, :, 128:1152] = pair(low_y[8:16], rows_at(15))

        left_ok = jnp.where(has_left, 1.0, 0.0)
        right_ok = jnp.where(has_right, 1.0, 0.0)
        down_ok = jnp.where(has_down, 1.0, 0.0)
        up_ok = jnp.where(has_up, 1.0, 0.0)

        def image_part(jb, _):
            here = pl.ds(pl.multiple_of(jb * 256, 128), 256)
            inner = pl.ds(pl.multiple_of(jb * 256 + 128, 128), 256)
            window = pl.ds(pl.multiple_of(jb * 256, 128), 512)
            total = dot(uc[:, window], wst[0, 0:512])
            total += dot(u[2:12, :, here].reshape(160, 256), wst[0, 512:768])
            total += dot(u[0:10, :, here].reshape(160, 256), wst[0, 768:1024])
            plus = shifted(uf, jb, 9, 0, 10)
            total += dot(plus.astype(BF), wst[0, 1024:1280])
            minus = shifted(uf, jb, 7, 0, 10)
            total += dot(minus.astype(BF), wst[0, 1280:1536])
            rounded = total.astype(BF).astype(F32)
            for x in range(10):
                part = rounded[x * 16:x * 16 + 16]
                if x == 0:
                    part = part * left_ok
                if x == 9:
                    part = part * right_ok
                imx[x * 16:x * 16 + 16, inner] = part.astype(BF)
                for k in range(2):
                    imf[2 * jb + k, x * 32 + 8:x * 32 + 24, :] = part[:, k * 128:k * 128 + 128]
            rim = dot(edge[0, :, window], wst[0, 0:512])
            for d in range(4):
                rim += dot(edge[d + 1, :, inner], wst[0, 512 + d * 256:768 + d * 256])
            rim = rim.astype(BF).astype(F32)
            for k in range(2):
                lanes = slice(k * 128, k * 128 + 128)
                imf[2 * jb + k, pl.ds(39, 8, stride=32), :] = rim[0:8, lanes] * down_ok
                imf[2 * jb + k, pl.ds(56, 8, stride=32), :] = rim[8:16, lanes] * up_ok
            return 0

        lax.fori_loop(0, 4, image_part, 0)

        def prior_part(jb, _):
            here = pl.ds(pl.multiple_of(jb * 256, 128), 256)
            inner = pl.ds(pl.multiple_of(jb * 256 + 128, 128), 256)
            window = pl.ds(pl.multiple_of(jb * 256, 128), 512)
            total = dot(imx[16:144, window], wst[1, 0:512])
            total += dot(imx[0:128, inner], wst[1, 512:768])
            total += dot(imx[32:160, inner], wst[1, 768:1024])
            minus = shifted(imf, jb, 7, 1, 9)
            total += dot(minus.astype(BF), wst[1, 1024:1280])
            plus = shifted(imf, jb, 9, 1, 9)
            total += dot(plus.astype(BF), wst[1, 1280:1536])
            prior[:, here] = total
            return 0

        lax.fori_loop(0, 4, prior_part, 0)

    def codes_in():
        remote(some, some, code_send.at[0], code_recv.at[0], (gy, right)).wait_recv()
        quarter = iota((1, 128), 1) // 32
        rows128 = iota((128, 128), 0)

        def hits(q, _):
            key = gotcode[4 * q]
            for o in range(1, 4):
                key = jnp.where(quarter == o, gotcode[4 * q + o], key)
            hit = jnp.where(rows128 == jnp.right_shift(key, 4), 1.0, 0.0).astype(BF).reshape(8, 16, 128)
            layer = jnp.broadcast_to(jnp.bitwise_and(key, 15), (16, 128))
            lanes = pl.ds(pl.multiple_of(q * 128, 128), 128)
            for z in range(16):
                only = jnp.where(layer == z, 1.0, 0.0).astype(BF)
                hot[z % 2, z // 2 * 128:z // 2 * 128 + 128, lanes] = (hit * only).reshape(128, 128)
            return 0

        lax.fori_loop(0, n // 4, hits, 0)

    low_lane = iota((size * 16, 128), 1) < 64

    def take(g):
        first = g * size
        part = got.at[pl.ds(first, size)] if g else got.at[pl.ds(1, size - 1)]
        remote(part, part, list_send.at[0], list_recv.at[g], (gy, right)).wait_recv()
        a = got[first:first + size, 0:16, :].astype(F32).reshape(size * 16, 128)
        w = got[first:first + size, 16:32, :].astype(F32).reshape(size * 16, 128)
        p = a * w
        hi = p.astype(BF).astype(F32)
        lo = p - hi
        wr, hir, lor = (pltpu.roll(v, 64, 1) for v in (w, hi, lo))
        for parity, slots, one, two in (
            (0, 0, jnp.where(low_lane, hi, wr), lo),
            (0, 1, jnp.where(low_lane, hir, w), lor),
            (1, 0, jnp.where(low_lane, w, hir), lor),
            (1, 1, jnp.where(low_lane, wr, hi), lo),
        ):
            at = slice(slots * 16, slots * 16 + 16)
            rhs[parity, first:first + size, at, 0:128] = one.astype(BF).reshape(size, 16, 128)
            rhs[parity, first:first + size, at, 128:256] = two.astype(BF).reshape(size, 16, 128)

    def add(start, stop):
        for parity in range(2):
            lists = rhs[parity, start * size:stop * size].reshape(-1, 256)
            part = dot(hot[parity, :, start * size * 32:stop * size * 32], lists)
            acc[parity] = part if start == 0 else acc[parity] + part

    some = gotcode.at[pl.ds(1, n - 1)]
    matrices()
    codes_in()
    take(0)
    beyond()
    take(1)
    take(3)
    take(2)
    add(0, ZS)

    low_out = iota((128, 128), 1) < 64
    puts = []
    for zz in range(8):
        rows = slice(zz * 128, zz * 128 + 128)
        even, odd = acc[0, rows], acc[1, rows]
        s1 = jnp.where(low_out, even[:, 0:128] + even[:, 128:256], odd[:, 0:128] + odd[:, 128:256])
        s0 = pltpu.roll(jnp.where(low_out, odd[:, 0:128], even[:, 0:128]), 64, 1)
        own = u[2:10, :, rows].astype(F32).reshape(128, 128)
        grad = s1 - own * s0 - prior[:, rows]
        res[:, :, rows] = grad.astype(BF).reshape(8, 16, 128)
        if zz % 2:
            put = pltpu.make_async_copy(
                res.at[:, :, pl.ds(zz * 128 - 128, 256)], out.at[:, :, pl.ds(zz * 128 - 128, 256)],
                out_sem.at[zz // 2],
            )
            put.start()
            puts.append(put)

    for k in range(8):
        halo(k, "wait_send")
    remote(some, some, code_send.at[0], code_recv.at[0], (gy, right)).wait_send()
    every = got.at[pl.ds(1, n - 1)]
    remote(every, every, list_send.at[0], list_recv.at[0], (gy, right)).wait_send()
    for put in puts:
        put.wait()


def on_device(field, center_block, couple_blocks, cell_index, slot_counts, assays, assay_weights):
    n, m = lax.axis_size("gx"), lax.axis_size("gy")
    vm, dma = pltpu.VMEM, pltpu.SemaphoreType.DMA
    i32 = jnp.int32
    return pl.pallas_call(
        functools.partial(kernel, n, m),
        out_shape=jax.ShapeDtypeStruct(field.shape, BF),
        in_specs=[pl.BlockSpec(memory_space=pltpu.HBM)] * 7,
        out_specs=pl.BlockSpec(memory_space=pltpu.HBM),
        scratch_shapes=[
            vm((12, 16, 1024), BF),
            vm((n, 2048), BF),
            vm((n, 2048), BF),
            vm((n, 32), i32),
            vm((1, n), i32),
            vm((64, 64), BF),
            vm((6, 64, 64), BF),
            vm((n * 16, 128), F32),
            vm((n, 32, 128), BF),
            vm((n, 32, 128), BF),
            vm((n, 1, 128), i32),
            vm((n, 1, 128), i32),
            vm((2, 16, 1024), BF),
            vm((2, 16, 1024), BF),
            vm((4, 8, 128), F32),
            vm((4, 8, 128), F32),
            vm((8, 320, 128), F32),
            vm((160, 1280), BF),
            vm((5, 16, 1280), BF),
            vm((8, 320, 128), F32),
            vm((160, 1280), BF),
            vm((2, 1536, 256), BF),
            vm((128, 1024), F32),
            vm((2, n, 32, 256), BF),
            vm((2, 1024, n * 32), BF),
            vm((2, 1024, 256), F32),
            vm((8, 16, 1024), BF),
            dma((7,)), dma((4,)), dma((8,)), dma((8,)),
            dma((1,)), dma((ZS,)), dma((1,)), dma((1,)),
        ],
        compiler_params=pltpu.CompilerParams(
            collective_id=0, has_side_effects=True, vmem_limit_bytes=56 * 1024 * 1024
        ),
    )(
        field, center_block, couple_blocks, cell_index.reshape(n, 32),
        slot_counts.reshape(1, n), assays.reshape(n, 2048), assay_weights.reshape(n, 2048),
    )


def solution(mesh):
    in_specs = (
        P("gx", "gy", None),
        P(),
        P(),
        P("gy", "gx", None, None),
        P("gy", "gx", None),
        P("gy", "gx", None, None),
        P("gy", "gx", None, None),
    )
    return jax.shard_map(
        on_device, mesh=mesh, in_specs=in_specs, out_specs=P("gx", "gy", None), check_vma=False
    )
```

```python
import functools

import jax
import jax.numpy as jnp
from jax import lax
from jax.experimental import pallas as pl
from jax.experimental.pallas import tpu as pltpu
from jax.sharding import PartitionSpec as P

BF = jnp.bfloat16
F32 = jnp.float32
MESH = pl.DeviceIdType.MESH
SENT = (0, 1, 3, 2)
ZS = 4


def dot(a, b):
    return jnp.dot(a, b, preferred_element_type=F32)


def dot_t(a, b):
    return lax.dot_general(a, b, (((1,), (1,)), ((), ())), preferred_element_type=F32)


def iota(shape, dim):
    return lax.broadcasted_iota(jnp.int32, shape, dim)


def put_wide(grid, row, values):
    for j in range(8):
        grid[j, row:row + values.shape[0], :] = values[:, j * 128:j * 128 + 128]


def put_column(grid, row, values):
    for j in range(8):
        grid[j, pl.ds(row, 8, stride=32), :] = values[:, j * 128:j * 128 + 128]


def get_column(grid, row):
    return jnp.concatenate([grid[j, pl.ds(row, 8, stride=32), :] for j in range(8)], axis=1)


def shifted(grid, jb, row, start, stop):
    return jnp.concatenate(
        [
            jnp.concatenate(
                [grid[2 * jb + k, x * 32 + row:x * 32 + row + 16, :] for x in range(start, stop)],
                axis=0,
            )
            for k in range(2)
        ],
        axis=1,
    )


def kernel(
    n, m,
    field, center, couple, index, counts, assays, weights,
    out,
    u, av, wv, iv, cv, kc, kd,
    stage, msg, got, code, gotcode,
    ysend, yrecv, csend, crecv,
    uf, uc, edge, imf, imx, wst, prior, rhs, hot, acc, res,
    in_sem, out_sem, halo_send, halo_recv, list_send, list_recv, code_send, code_recv,
):
    gy, gx = lax.axis_index("gy"), lax.axis_index("gx")
    left, right = lax.rem(gx + n - 1, n), lax.rem(gx + 1, n)
    down, up = lax.rem(gy + m - 1, m), lax.rem(gy + 1, m)

    ins = [
        pltpu.make_async_copy(assays, av, in_sem.at[0]),
        pltpu.make_async_copy(weights, wv, in_sem.at[1]),
        pltpu.make_async_copy(field, u.at[pl.ds(2, 8)], in_sem.at[2]),
        pltpu.make_async_copy(index, iv, in_sem.at[3]),
        pltpu.make_async_copy(counts, cv, in_sem.at[4]),
        pltpu.make_async_copy(center, kc, in_sem.at[5]),
        pltpu.make_async_copy(couple, kd, in_sem.at[6]),
    ]
    for one in ins:
        one.start()

    size = n // ZS
    barrier = pltpu.get_barrier_semaphore()

    def greet(d, _):
        pl.semaphore_signal(
            barrier, inc=1, device_id=(gy, lax.rem(gx + d, n)), device_id_type=MESH
        )
        return 0

    lax.fori_loop(1, n, greet, 0)
    has_left, has_right, has_down, has_up = gx > 0, gx < n - 1, gy > 0, gy < m - 1
    beside = (
        (has_down, (down, gx)), (has_up, (up, gx)),
        (has_down & has_left, (down, left)), (has_down & has_right, (down, right)),
        (has_up & has_left, (up, left)), (has_up & has_right, (up, right)),
    )
    greetings = n - 1
    for there, who in beside:
        greetings += jnp.where(there, 1, 0)

        @pl.when(there)
        def _(who=who):
            pl.semaphore_signal(barrier, inc=1, device_id=who, device_id_type=MESH)

    for which, (copy, src) in enumerate(((ins[0], av), (ins[1], wv))):
        copy.wait()
        for j in range(16):
            stage[pl.ds(j, n, stride=16), :] = src[:, j * 128:(j + 1) * 128].astype(F32)
        msg[:, which * 16:(which + 1) * 16, :] = stage[0:n * 16, :].reshape(n, 16, 128).astype(BF)

    ins[3].wait()
    ins[4].wait()
    row, lane = iota((n, n), 0), iota((n, n), 1)
    count = jnp.sum(jnp.where(row == lane, cv[...].astype(F32), 0.0), axis=1, keepdims=True)
    used = iota((n, 32), 1).astype(F32) < count
    cells = jnp.where(used, iv[...], -1)
    pick_s, pick_l = iota((32, 128), 0), iota((32, 128), 1)
    pick = jnp.where(
        pick_s == 2 * lax.rem(pick_l, 16) + lax.rem(pick_l, 32) // 16, 1.0, 0.0
    ).astype(BF)
    high = dot(jnp.right_shift(cells, 4).astype(F32).astype(BF), pick)
    low = dot(jnp.bitwise_and(cells, 15).astype(F32).astype(BF), pick)
    codes = (high * 16.0 + low).astype(jnp.int32)
    for t in range(n):
        code[t] = codes[t:t + 1]

    ins[2].wait()
    for x in range(8):
        put_wide(uf, (x + 1) * 32 + 8, u[x + 2].astype(F32))

    def rows_at(y):
        return get_column(uf, 40 + y)

    ysend[0] = jnp.concatenate([rows_at(0), rows_at(1)], axis=0).astype(BF)
    ysend[1] = jnp.concatenate([rows_at(15), rows_at(14)], axis=0).astype(BF)
    for c, (x, y) in enumerate(((7, 15), (7, 0), (0, 15), (0, 0))):
        place = (x + 1) * 32 + 8 + y
        for j in range(8):
            csend[c, j:j + 1, :] = uf[j, place:place + 1, :]

    pl.semaphore_wait(barrier, greetings)

    def remote(src, dst, send, recv, who):
        return pltpu.make_async_remote_copy(
            src_ref=src, dst_ref=dst, send_sem=send, recv_sem=recv,
            device_id=who, device_id_type=MESH,
        )

    halos = [
        (has_left, has_right, u.at[pl.ds(2, 2)], u.at[pl.ds(10, 2)], (gy, left)),
        (has_right, has_left, u.at[pl.ds(8, 2)], u.at[pl.ds(0, 2)], (gy, right)),
        (has_down, has_up, ysend.at[0], yrecv.at[1], (down, gx)),
        (has_up, has_down, ysend.at[1], yrecv.at[0], (up, gx)),
        (has_up & has_right, has_down & has_left, csend.at[0], crecv.at[0], (up, right)),
        (has_down & has_right, has_up & has_left, csend.at[1], crecv.at[1], (down, right)),
        (has_up & has_left, has_down & has_right, csend.at[2], crecv.at[2], (up, left)),
        (has_down & has_left, has_up & has_right, csend.at[3], crecv.at[3], (down, left)),
    ]

    def halo(k, what):
        sends, receives, src, dst, who = halos[k]
        copy = remote(src, dst, halo_send.at[k], halo_recv.at[k], who)

        @pl.when(receives if what == "wait_recv" else sends)
        def _():
            getattr(copy, what)()

    for k in range(8):
        halo(k, "start")

    def partner(g, k):
        y, z, c = gx // 8 + k // 2, lax.rem(gx // 2, ZS) + g, lax.rem(gx, 2) + lax.rem(k, 2)
        return lax.rem(y, n // 8) * 8 + lax.rem(z, ZS) * 2 + lax.rem(c, 2)

    def send_code(g, k):
        to = partner(g, k)
        remote(code.at[to], gotcode.at[g * size + k], code_send.at[0], code_recv.at[0], (gy, to)).start()

    def send_list(g, k):
        to = partner(g, k)
        remote(msg.at[to], got.at[g * size + k], list_send.at[0], list_recv.at[g], (gy, to)).start()

    for send in (send_code, send_list):
        for g in SENT:

            def each(k, _, g=g, send=send):
                send(g, k)
                return 0

            lax.fori_loop(1 if g == 0 else 0, size, each, 0)
    got[0] = msg[gx]
    gotcode[0] = code[gx]

    def matrices():
        ins[5].wait()
        ins[6].wait()
        spread = jnp.where(lax.rem(iota((256, 64), 0), 64) == iota((256, 64), 1), 1.0, 0.0).astype(BF)
        rb, cb = iota((256, 256), 0) // 64, iota((256, 256), 1) // 64

        def tiled(block, flip):
            tall = (dot_t if flip else dot)(spread, block).astype(BF)
            return dot_t(tall, spread)

        for s in range(2):
            mid = tiled(kc[...], s == 1)
            above = tiled(kd[5 if s else 4], s == 1)
            below = tiled(kd[4 if s else 5], s == 1)
            for half in range(2):
                zr = rb - 2 + 4 * half
                window = jnp.where(zr == cb, mid, 0.0)
                window = jnp.where(zr == cb + 1, -above, window)
                window = jnp.where(zr == cb - 1, -below, window)
                wst[s, half * 256:half * 256 + 256, :] = window.astype(BF)
            for d in range(4):
                wst[s, 512 + d * 256:768 + d * 256, :] = jnp.where(
                    rb == cb, -tiled(kd[d], s == 1), 0.0
                ).astype(BF)

    def beyond():
        for k in range(8):
            halo(k, "wait_recv")
        zero = jnp.zeros((), F32)
        for slot, ok in ((0, has_left), (10, has_right)):
            for x in (slot, slot + 1):
                u[x] = jnp.where(ok, u[x].astype(F32), zero).astype(BF)
        put_wide(uf, 8, u[1].astype(F32))
        put_wide(uf, 9 * 32 + 8, u[10].astype(F32))
        low_y = jnp.where(has_down, yrecv[0].astype(F32), zero)
        high_y = jnp.where(has_up, yrecv[1].astype(F32), zero)
        put_column(uf, 32 + 7, low_y[0:8])
        put_column(uf, 32 + 24, high_y[0:8])
        for c, (x, y, ok) in enumerate(
            ((-1, -1, has_left & has_down), (-1, 16, has_left & has_up),
             (8, -1, has_right & has_down), (8, 16, has_right & has_up))
        ):
            place = (x + 1) * 32 + 8 + y
            for j in range(8):
                uf[j, place:place + 1, :] = jnp.where(ok, crecv[c, j:j + 1, :], zero)
        uc[:, 0:128] = jnp.zeros((160, 128), BF)
        uc[:, 1152:1280] = jnp.zeros((160, 128), BF)
        imx[:, 0:128] = jnp.zeros((160, 128), BF)
        imx[:, 1152:1280] = jnp.zeros((160, 128), BF)
        edge[:, :, 0:128] = jnp.zeros((5, 16, 128), BF)
        edge[:, :, 1152:1280] = jnp.zeros((5, 16, 128), BF)
        for x in range(10):
            uc[x * 16:x * 16 + 16, 128:1152] = u[x + 1]

        def pair(first, second):
            return jnp.concatenate([first, second], axis=0).astype(BF)

        edge[0, :, 128:1152] = pair(low_y[0:8], high_y[0:8])
        edge[1, :, 128:1152] = pair(get_column(uf, 64 + 7), get_column(uf, 64 + 24))
        edge[2, :, 128:1152] = pair(get_column(uf, 7), get_column(uf, 24))
        edge[3, :, 128:1152] = pair(rows_at(0), high_y[8:16])
        edge[4, :, 128:1152] = pair(low_y[8:16], rows_at(15))

        left_ok = jnp.where(has_left, 1.0, 0.0)
        right_ok = jnp.where(has_right, 1.0, 0.0)
        down_ok = jnp.where(has_down, 1.0, 0.0)
        up_ok = jnp.where(has_up, 1.0, 0.0)

        def image_part(jb, _):
            here = pl.ds(pl.multiple_of(jb * 256, 128), 256)
            inner = pl.ds(pl.multiple_of(jb * 256 + 128, 128), 256)
            window = pl.ds(pl.multiple_of(jb * 256, 128), 512)
            total = dot(uc[:, window], wst[0, 0:512])
            total += dot(u[2:12, :, here].reshape(160, 256), wst[0, 512:768])
            total += dot(u[0:10, :, here].reshape(160, 256), wst[0, 768:1024])
            plus = shifted(uf, jb, 9, 0, 10)
            total += dot(plus.astype(BF), wst[0, 1024:1280])
            minus = shifted(uf, jb, 7, 0, 10)
            total += dot(minus.astype(BF), wst[0, 1280:1536])
            rounded = total.astype(BF).astype(F32)
            for x in range(10):
                part = rounded[x * 16:x * 16 + 16]
                if x == 0:
                    part = part * left_ok
                if x == 9:
                    part = part * right_ok
                imx[x * 16:x * 16 + 16, inner] = part.astype(BF)
                for k in range(2):
                    imf[2 * jb + k, x * 32 + 8:x * 32 + 24, :] = part[:, k * 128:k * 128 + 128]
            rim = dot(edge[0, :, window], wst[0, 0:512])
            for d in range(4):
                rim += dot(edge[d + 1, :, inner], wst[0, 512 + d * 256:768 + d * 256])
            rim = rim.astype(BF).astype(F32)
            for k in range(2):
                lanes = slice(k * 128, k * 128 + 128)
                imf[2 * jb + k, pl.ds(39, 8, stride=32), :] = rim[0:8, lanes] * down_ok
                imf[2 * jb + k, pl.ds(56, 8, stride=32), :] = rim[8:16, lanes] * up_ok
            return 0

        lax.fori_loop(0, 4, image_part, 0)

        def prior_part(jb, _):
            here = pl.ds(pl.multiple_of(jb * 256, 128), 256)
            inner = pl.ds(pl.multiple_of(jb * 256 + 128, 128), 256)
            window = pl.ds(pl.multiple_of(jb * 256, 128), 512)
            total = dot(imx[16:144, window], wst[1, 0:512])
            total += dot(imx[0:128, inner], wst[1, 512:768])
            total += dot(imx[32:160, inner], wst[1, 768:1024])
            minus = shifted(imf, jb, 7, 1, 9)
            total += dot(minus.astype(BF), wst[1, 1024:1280])
            plus = shifted(imf, jb, 9, 1, 9)
            total += dot(plus.astype(BF), wst[1, 1280:1536])
            prior[:, here] = total
            return 0

        lax.fori_loop(0, 4, prior_part, 0)

    def codes_in():
        remote(some, some, code_send.at[0], code_recv.at[0], (gy, right)).wait_recv()
        quarter = iota((1, 128), 1) // 32
        rows128 = iota((128, 128), 0)

        def hits(q, _):
            key = gotcode[4 * q]
            for o in range(1, 4):
                key = jnp.where(quarter == o, gotcode[4 * q + o], key)
            hit = jnp.where(rows128 == jnp.right_shift(key, 4), 1.0, 0.0).astype(BF).reshape(8, 16, 128)
            layer = jnp.broadcast_to(jnp.bitwise_and(key, 15), (16, 128))
            lanes = pl.ds(pl.multiple_of(q * 128, 128), 128)
            for z in range(16):
                only = jnp.where(layer == z, 1.0, 0.0).astype(BF)
                hot[z % 2, z // 2 * 128:z // 2 * 128 + 128, lanes] = (hit * only).reshape(128, 128)
            return 0

        lax.fori_loop(0, n // 4, hits, 0)

    low_lane = iota((size * 16, 128), 1) < 64

    def take(g):
        first = g * size
        part = got.at[pl.ds(first, size)] if g else got.at[pl.ds(1, size - 1)]
        remote(part, part, list_send.at[0], list_recv.at[g], (gy, right)).wait_recv()
        a = got[first:first + size, 0:16, :].astype(F32).reshape(size * 16, 128)
        w = got[first:first + size, 16:32, :].astype(F32).reshape(size * 16, 128)
        p = a * w
        hi = p.astype(BF).astype(F32)
        lo = p - hi
        wr, hir, lor = (pltpu.roll(v, 64, 1) for v in (w, hi, lo))
        for parity, slots, one, two in (
            (0, 0, jnp.where(low_lane, hi, wr), lo),
            (0, 1, jnp.where(low_lane, hir, w), lor),
            (1, 0, jnp.where(low_lane, w, hir), lor),
            (1, 1, jnp.where(low_lane, wr, hi), lo),
        ):
            at = slice(slots * 16, slots * 16 + 16)
            rhs[parity, first:first + size, at, 0:128] = one.astype(BF).reshape(size, 16, 128)
            rhs[parity, first:first + size, at, 128:256] = two.astype(BF).reshape(size, 16, 128)

    def add(start, stop):
        for parity in range(2):
            lists = rhs[parity, start * size:stop * size].reshape(-1, 256)
            part = dot(hot[parity, :, start * size * 32:stop * size * 32], lists)
            acc[parity] = part if start == 0 else acc[parity] + part

    some = gotcode.at[pl.ds(1, n - 1)]
    matrices()
    codes_in()
    take(0)
    beyond()
    take(1)
    take(3)
    take(2)
    add(0, ZS)

    low_out = iota((128, 128), 1) < 64
    puts = []
    for zz in range(8):
        rows = slice(zz * 128, zz * 128 + 128)
        even, odd = acc[0, rows], acc[1, rows]
        s1 = jnp.where(low_out, even[:, 0:128] + even[:, 128:256], odd[:, 0:128] + odd[:, 128:256])
        s0 = pltpu.roll(jnp.where(low_out, odd[:, 0:128], even[:, 0:128]), 64, 1)
        own = u[2:10, :, rows].astype(F32).reshape(128, 128)
        grad = s1 - own * s0 - prior[:, rows]
        res[:, :, rows] = grad.astype(BF).reshape(8, 16, 128)
        if zz % 2:
            put = pltpu.make_async_copy(
                res.at[:, :, pl.ds(zz * 128 - 128, 256)], out.at[:, :, pl.ds(zz * 128 - 128, 256)],
                out_sem.at[zz // 2],
            )
            put.start()
            puts.append(put)

    for k in range(8):
        halo(k, "wait_send")
    remote(some, some, code_send.at[0], code_recv.at[0], (gy, right)).wait_send()
    every = got.at[pl.ds(1, n - 1)]
    remote(every, every, list_send.at[0], list_recv.at[0], (gy, right)).wait_send()
    for put in puts:
        put.wait()


def on_device(field, center_block, couple_blocks, cell_index, slot_counts, assays, assay_weights):
    n, m = lax.axis_size("gx"), lax.axis_size("gy")
    vm, dma = pltpu.VMEM, pltpu.SemaphoreType.DMA
    i32 = jnp.int32
    return pl.pallas_call(
        functools.partial(kernel, n, m),
        out_shape=jax.ShapeDtypeStruct(field.shape, BF),
        in_specs=[pl.BlockSpec(memory_space=pltpu.HBM)] * 7,
        out_specs=pl.BlockSpec(memory_space=pltpu.HBM),
        scratch_shapes=[
            vm((12, 16, 1024), BF),
            vm((n, 2048), BF),
            vm((n, 2048), BF),
            vm((n, 32), i32),
            vm((1, n), i32),
            vm((64, 64), BF),
            vm((6, 64, 64), BF),
            vm((n * 16 + 16, 128), F32),
            vm((n, 32, 128), BF),
            vm((n, 32, 128), BF),
            vm((n, 1, 128), i32),
            vm((n, 1, 128), i32),
            vm((2, 16, 1024), BF),
            vm((2, 16, 1024), BF),
            vm((4, 8, 128), F32),
            vm((4, 8, 128), F32),
            vm((8, 384, 128), F32),
            vm((160, 1280), BF),
            vm((5, 16, 1280), BF),
            vm((8, 384, 128), F32),
            vm((160, 1280), BF),
            vm((2, 1536, 256), BF),
            vm((128, 1024), F32),
            vm((2, n, 32, 256), BF),
            vm((2, 1024, n * 32), BF),
            vm((2, 1024, 256), F32),
            vm((8, 16, 1024), BF),
            dma((7,)), dma((4,)), dma((8,)), dma((8,)),
            dma((1,)), dma((ZS,)), dma((1,)), dma((1,)),
        ],
        compiler_params=pltpu.CompilerParams(
            collective_id=0, has_side_effects=True, vmem_limit_bytes=56 * 1024 * 1024
        ),
    )(
        field, center_block, couple_blocks, cell_index.reshape(n, 32),
        slot_counts.reshape(1, n), assays.reshape(n, 2048), assay_weights.reshape(n, 2048),
    )


def solution(mesh):
    in_specs = (
        P("gx", "gy", None),
        P(),
        P(),
        P("gy", "gx", None, None),
        P("gy", "gx", None),
        P("gy", "gx", None, None),
        P("gy", "gx", None, None),
    )
    return jax.shard_map(
        on_device, mesh=mesh, in_specs=in_specs, out_specs=P("gx", "gy", None), check_vma=False
    )
```
